256 devices in a mesh: dp: 2 (over core), mp: 128 (over z, y, x).
Axes of the slice: x: 4, y: 4, z: 8, core: 2. Of those that a mesh axis runs over, the one named last changes fastest.
Arguments:
- grad_parts: bfloat16 [2, 1536, 65536], P('dp', None, 'mp'), may hold values from -8000 to 8000
- owner: int32 [128, 3], P('mp'), may hold values from 0 to 1, as said below
- row_block: int32 [128, 3], P('mp'), may hold values from 0 to 2, as said below
- left_stats: float32 [128, 4, 512, 512], P('mp', 'dp'), may hold values from -1 to 6
- right_stats: float32 [128, 4, 512, 512], P('mp', 'dp'), may hold values from -1 to 6
- left_root: bfloat16 [128, 4, 512, 512], P('mp', 'dp'), may hold values from -1 to 6
- right_root: bfloat16 [128, 4, 512, 512], P('mp', 'dp'), may hold values from -1 to 6
- row_moment: float32 [128, 4, 512], P('mp', 'dp'), may hold values from 0.3 to 3
- col_moment: float32 [128, 4, 512], P('mp', 'dp'), may hold values from 0.3 to 3
Outputs:
- direction: bfloat16 [1536, 65536], P('dp', 'mp')
- new_left: float32 [128, 4, 512, 512], P('mp', 'dp')
- new_right: float32 [128, 4, 512, 512], P('mp', 'dp')
- new_rows: float32 [128, 4, 512], P('mp', 'dp')
- new_cols: float32 [128, 4, 512], P('mp', 'dp')
The draws below stay inside these ranges and needn't reach their ends.
Inputs may be any that keep to these rules, and one draw needn't show every extreme that they name: In each column shard's list, every owner is named by at most 2 entries, and one owner by exactly 2. `row_block`: each column shard's list names every row block exactly once.
All inputs are finite; a program needn't handle non-finite values.
Results may differ from the reference program's by a relative error of at most 0.0058.
Values may be sent and summed in bfloat16 or wider, within the bound.
No kernel may reach another device: no remote copies, remote signals or barrier semaphores. Data moves between devices by JAX's collectives and lax.ppermute only.
A program may use at most 64 MiB of HBM per device.

```python
import math
import jax
import jax.numpy as jnp
from jax import lax

B = 512
CAP = 2
BLK = 3
ROWS = 1536
COLS = 65536
SLOTS = 4
N_DP = 2
N_MP = 128


def symmetric_draw(key, leading, order_n, low_end, high_end, spread):
    key_diag, key_noise = jax.random.split(key)
    diagonal = jnp.exp(jax.random.uniform(key_diag, leading + (order_n,), jnp.float32, math.log(low_end), math.log(high_end)))
    noise_part = jax.random.normal(key_noise, leading + (order_n, order_n), jnp.float32)
    noise_part = (noise_part + jnp.swapaxes(noise_part, -1, -2)) * (spread / math.sqrt(2.0))
    positions = jnp.arange(order_n)
    identity = (positions[:, None] == positions[None, :]).astype(jnp.float32)
    result = noise_part * (1.0 - identity) + identity * diagonal[..., :, None]
    return jnp.clip(result, -1.0, 6.0)


def owner_and_rows(key):
    owner_key = jax.random.fold_in(key, 31)
    order_key = jax.random.fold_in(key, 41)

    def single_row(row_key):
        key_heavy, key_other, key_order = jax.random.split(row_key, 3)
        heavy_owner = jax.random.randint(key_heavy, (), 0, N_DP)
        other_owners = jax.random.permutation(key_other, N_DP - 1)
        entry_ids = jnp.arange(BLK, dtype=jnp.int32)
        rest_owners = (heavy_owner + 1 + other_owners[jnp.maximum(entry_ids - CAP, 0) % (N_DP - 1)]) % N_DP
        base_list = jnp.where(entry_ids < CAP, heavy_owner, rest_owners)
        return jax.random.permutation(key_order, base_list)

    def single_order(row_key):
        return jax.random.permutation(row_key, BLK)
    owners = jax.vmap(single_row)(jax.random.split(owner_key, N_MP)).astype(jnp.int32)
    orders = jax.vmap(single_order)(jax.random.split(order_key, N_MP)).astype(jnp.int32)
    return (owners, orders)


def draw_grad_parts(key, part):
    owners, orders = owner_and_rows(key)
    key = jax.random.fold_in(key, 21)
    key_base = jax.random.fold_in(key, 0)
    key_rows = jax.random.fold_in(key, 1)
    key_cols = jax.random.fold_in(key, 2)
    key_shard = jax.random.fold_in(key, 5)
    column_ramp = jnp.arange(COLS, dtype=jnp.float32) / max(COLS - 1, 1)
    shard_factor = jnp.exp(jax.random.uniform(key_shard, (N_MP,), jnp.float32, 0.0, math.log(10.0)))
    shard_columns = jnp.broadcast_to(shard_factor[:, None], (N_MP, B)).reshape(COLS)
    base_draw = jnp.clip(jax.random.normal(key_base, (N_DP, ROWS, COLS), jnp.float32), -4.0, 4.0)
    rows_scale = jnp.exp(jax.random.uniform(key_rows, (ROWS,), jnp.float32, 0.0, math.log(6.0)))
    cols_scale = jnp.exp(jax.random.uniform(key_cols, (COLS,), jnp.float32, 0.0, math.log(3.3))) * jnp.exp(math.log(3.0) * column_ramp)
    cols_scale = cols_scale * shard_columns
    owner_factor = jnp.exp(math.log(3.0) * owners.astype(jnp.float32) / max(N_DP - 1, 1))
    onehot = (orders[:, :, None] == jnp.arange(BLK, dtype=jnp.int32)[None, None, :]).astype(jnp.float32)
    block_scale = jnp.sum(owner_factor[:, :, None] * onehot, axis=1)
    block_field = jnp.broadcast_to(block_scale.T[:, None, :, None], (BLK, B, N_MP, B)).reshape(ROWS, COLS)
    gradient = base_draw * rows_scale[None, :, None] * cols_scale[None, None, :] * block_field[None, :, :]
    return jnp.clip(gradient, -8000.0, 8000.0).astype(jnp.bfloat16)


def draw_owner(key, part):
    owners, orders = owner_and_rows(key)
    return owners


def draw_row_block(key, part):
    owners, orders = owner_and_rows(key)
    return orders


def draw_left_stats(key, part):
    key = jax.random.fold_in(key, 11)
    return symmetric_draw(key, (N_MP, SLOTS), B, 0.5, 2.0, 0.02)


def draw_right_stats(key, part):
    key = jax.random.fold_in(key, 12)
    return symmetric_draw(key, (N_MP, SLOTS), B, 0.5, 2.0, 0.02)


def draw_left_root(key, part):
    key = jax.random.fold_in(key, 13)
    return symmetric_draw(key, (N_MP, SLOTS), B, 0.5, 2.0, 0.02).astype(jnp.bfloat16)


def draw_right_root(key, part):
    key = jax.random.fold_in(key, 14)
    return symmetric_draw(key, (N_MP, SLOTS), B, 0.5, 2.0, 0.02).astype(jnp.bfloat16)


def level_of(rng, extent, shards, smallest, high):
    loudness = 1.0
    for dim, blocks in shards:
        heights = jax.random.uniform(jax.random.fold_in(jax.random.fold_in(rng, 6), dim), (blocks,), jnp.float32, smallest / len(shards), high / len(shards))
        loudness = loudness * jnp.repeat(jnp.exp(heights), extent[dim] // blocks).reshape((-1,) + (1,) * (len(extent) - 1 - dim))
    return loudness


def setup_inputs(seed: int = 0) -> dict:
    key_of = jax.random.split(jax.random.key(seed), 10)
    grad_parts = draw_grad_parts(jax.random.fold_in(key_of[9], 71), 0)
    owner = draw_owner(jax.random.fold_in(key_of[9], 71), 0)
    row_block = draw_row_block(jax.random.fold_in(key_of[9], 71), 0)
    left_stats = draw_left_stats(jax.random.fold_in(key_of[9], 71), 0)
    right_stats = draw_right_stats(jax.random.fold_in(key_of[9], 71), 0)
    left_root = draw_left_root(jax.random.fold_in(key_of[9], 71), 0)
    right_root = draw_right_root(jax.random.fold_in(key_of[9], 71), 0)
    row_moment = jnp.clip(jnp.exp(math.log(3.0) - 2.3025851 * jax.random.uniform(key_of[7], (N_MP, SLOTS, B), jnp.float32) ** level_of(key_of[7], (N_MP, SLOTS, B), ((0, 128), (1, 2)), -0.2, 0.2)), 0.3, 3.0)
    col_moment = jnp.clip(jnp.exp(math.log(3.0) - 2.3025851 * jax.random.uniform(key_of[8], (N_MP, SLOTS, B), jnp.float32) ** level_of(key_of[8], (N_MP, SLOTS, B), ((0, 128), (1, 2)), -0.2, 0.2)), 0.3, 3.0)
    return dict(grad_parts=grad_parts, owner=owner, row_block=row_block, left_stats=left_stats, right_stats=right_stats, left_root=left_root, right_root=right_root, row_moment=row_moment, col_moment=col_moment)


DECAY_RATE = 0.95
PRECISE = lax.Precision.HIGHEST

def slot_numbers(owner_row, capacity):
    entry_count = owner_row.shape[0]
    positions = jnp.arange(entry_count, dtype=jnp.int32)
    earlier = positions[None, :] < positions[:, None]
    same_owner = owner_row[None, :] == owner_row[:, None]
    before = lax.optimization_barrier(jnp.sum(jnp.where(earlier & same_owner, 1, 0).astype(jnp.int32), axis=1))
    return (owner_row * capacity + before).astype(jnp.int32)

def single_block(inputs):
    blocks, old_left, old_right, left_root, right_root, old_rows, old_cols = inputs
    stat_mix = (1.0 - DECAY_RATE) / B
    left_new = DECAY_RATE * old_left + stat_mix * jnp.dot(blocks, blocks.T, precision=PRECISE)
    right_new = DECAY_RATE * old_right + stat_mix * jnp.dot(blocks.T, blocks, precision=PRECISE)
    squares = blocks * blocks
    rows_new = DECAY_RATE * old_rows + (1.0 - DECAY_RATE) * lax.optimization_barrier(jnp.mean(squares, axis=1))
    cols_new = DECAY_RATE * old_cols + (1.0 - DECAY_RATE) * lax.optimization_barrier(jnp.mean(squares, axis=0))
    second = rows_new[:, None] * cols_new[None, :] / jnp.mean(rows_new)
    adam_step = blocks / (jnp.sqrt(second) + 1e-08)
    rounded = blocks.astype(jnp.bfloat16)
    half_done = jnp.dot(left_root, rounded, preferred_element_type=jnp.float32).astype(jnp.bfloat16)
    precond = jnp.dot(half_done, right_root, preferred_element_type=jnp.float32)
    graft_ratio = jnp.sqrt(jnp.mean(adam_step * adam_step)) / jnp.sqrt(jnp.mean(precond * precond) + 1e-06)
    update = (-graft_ratio * precond).astype(jnp.bfloat16)
    return (left_new, right_new, rows_new, cols_new, update)

def reference(grad_parts, owner, row_block, left_stats, right_stats, left_root, right_root, row_moment, col_moment):
    summed = jnp.zeros((ROWS, COLS), jnp.float32)
    for replica in range(N_DP):
        summed = summed + grad_parts[replica].astype(jnp.float32)
    total_sq = jnp.sum(summed * summed)
    clip_factor = 1.0 / jnp.sqrt(total_sq / (ROWS * COLS) + 1e-06)
    columns = jnp.transpose(summed.reshape(ROWS, N_MP, B), (1, 0, 2))

    def single_shard(inputs):
        column, owner_row, rows_row, left, right, lroot, rroot, rmom, cmom = inputs
        slot_ids = slot_numbers(owner_row, CAP)
        blocks = column.reshape(BLK, B, B)[rows_row] * clip_factor
        results = lax.map(single_block, (blocks, left[slot_ids], right[slot_ids], lroot[slot_ids], rroot[slot_ids], rmom[slot_ids], cmom[slot_ids]))
        left_new, right_new, rows_new, cols_new, update = results
        shard_dir = jnp.zeros((BLK, B, B), jnp.bfloat16).at[rows_row].set(update).reshape(BLK * B, B)
        return (shard_dir, left.at[slot_ids].set(left_new), right.at[slot_ids].set(right_new), rmom.at[slot_ids].set(rows_new), cmom.at[slot_ids].set(cols_new))
    shard_dirs, left_all, right_all, rows_all, cols_all = lax.map(single_shard, (columns, owner, row_block, left_stats, right_stats, left_root, right_root, row_moment, col_moment))
    direction = jnp.transpose(shard_dirs, (1, 0, 2)).reshape(ROWS, COLS)
    return (direction, left_all, right_all, rows_all, cols_all)
```

```python
import functools

import jax
import jax.numpy as jnp
from jax import lax
from jax.experimental import pallas as pl
from jax.experimental.pallas import tpu as pltpu
from jax.sharding import PartitionSpec as P

DECAY = 0.95
SCALE = 1024.0
B = 512
BLK = 3
CAP = 2
HALF = B // 2
F32 = jnp.float32
BF16 = jnp.bfloat16
SWAP = [(0, 1), (1, 0)]
MIB = 1 << 20
VM = pl.BlockSpec(memory_space=pltpu.VMEM)
SM = pl.BlockSpec(memory_space=pltpu.SMEM)
HB = pl.BlockSpec(memory_space=pltpu.HBM)


def lanes_sum(x):
    return x[:, 0:128] + x[:, 128:256] + x[:, 256:384] + x[:, 384:512]


def scaled_sum(a, b):
    return (a.astype(F32) + b.astype(F32)) * SCALE


def square_kernel(g_ref, o_ref, out_ref):
    step = 64

    def body(i, acc):
        rows = pl.ds(pl.multiple_of(i * step, step), step)
        s = scaled_sum(g_ref[rows, :], o_ref[rows, :])
        s = s * s
        return acc + jnp.sum(s.reshape(step // 8, 8, B), axis=0)

    acc = lax.fori_loop(0, BLK * B // step, body, jnp.zeros((8, B), F32), unroll=4)
    out_ref[...] = jnp.sum(lanes_sum(acc), axis=0, keepdims=True)


def square_sum(g, o):
    return pl.pallas_call(
        square_kernel,
        out_shape=pltpu.VMEM((1, 128), F32),
        in_specs=[VM, VM],
        out_specs=VM,
        compiler_params=pltpu.CompilerParams(vmem_limit_bytes=8 * MIB),
        cost_estimate=pl.CostEstimate(
            flops=4 * BLK * B * B, bytes_accessed=4 * BLK * B * B, transcendentals=0
        ),
        name="squares",
    )(g, o)


def load_kernel(g_hbm, lroot_hbm, rroot_hbm, left_hbm, right_hbm, rows_hbm, cols_hbm,
                g_ref, lroot_ref, rroot_ref, left_ref, right_ref, moment_ref, rows_ref, cols_ref, sems):
    pairs = (
        (rows_hbm, rows_ref), (cols_hbm, cols_ref), (g_hbm, g_ref), (lroot_hbm, lroot_ref), (rroot_hbm, rroot_ref),
        (left_hbm, left_ref), (right_hbm, right_ref),
    )
    copies = [pltpu.make_async_copy(a, b, sems.at[i]) for i, (a, b) in enumerate(pairs)]
    for c in copies:
        c.start()
    for c in copies:
        c.wait()
    moment_ref[0:2, :] = rows_ref[...]
    moment_ref[2:4, :] = cols_ref[...]


def load(g, lroot, rroot, left, right, rows, cols):
    return pl.pallas_call(
        load_kernel,
        out_shape=(
            pltpu.VMEM((BLK * B, B), BF16),
            pltpu.VMEM((CAP, B, B), BF16),
            pltpu.VMEM((CAP, B, B), BF16),
            pltpu.VMEM((CAP, B, B), F32),
            pltpu.VMEM((CAP, B, B), F32),
            pltpu.VMEM((4, B), F32),
        ),
        in_specs=[HB] * 7,
        out_specs=(VM,) * 6,
        scratch_shapes=[
            pltpu.VMEM((CAP, B), F32),
            pltpu.VMEM((CAP, B), F32),
            pltpu.SemaphoreType.DMA((7,)),
        ],
        compiler_params=pltpu.CompilerParams(vmem_limit_bytes=2 * MIB),
        cost_estimate=pl.CostEstimate(flops=0, bytes_accessed=8 * MIB, transcendentals=0),
        name="load",
    )(*[pltpu.with_memory_space_constraint(a, pltpu.HBM) for a in (g, lroot, rroot, left, right, rows, cols)])


def slot_of_entry(owner_ref):
    o0, o1, o2 = owner_ref[0, 0], owner_ref[0, 1], owner_ref[0, 2]
    one = jnp.int32(1)
    zero = jnp.int32(0)
    s1 = jnp.where(o1 == o0, one, zero)
    s2 = jnp.where(o2 == o0, one, zero) + jnp.where(o2 == o1, one, zero)
    return (o0, o1, o2), (zero, s1, s2)


def rows_of_slots(owner_ref, row_ref, me):
    owners, slots = slot_of_entry(owner_ref)
    found = []
    for s in range(CAP):
        row, filled = jnp.int32(0), jnp.int32(0)
        for k in range(BLK):
            hit = (owners[k] == me) & (slots[k] == s)
            row = jnp.where(hit, row_ref[0, k], row)
            filled = jnp.where(hit, jnp.int32(1), filled)
        found.append((row, filled))
    return found


def entry_of_blocks(owner_ref, row_ref, me):
    owners, slots = slot_of_entry(owner_ref)
    found = []
    for b in range(BLK):
        mine, slot = jnp.int32(0), jnp.int32(0)
        for k in range(BLK):
            hit = row_ref[0, k] == b
            mine = jnp.where(hit & (owners[k] == me), jnp.int32(1), mine)
            slot = jnp.where(hit, slots[k], slot)
        found.append((mine, slot))
    return found


def product_kernel(owner_ref, row_ref, g_ref, o_ref, lroot_ref, rroot_ref, _, mine_ref, send_ref, psq_ref, tick_ref):
    me = lax.axis_index("dp")
    tick_ref[...] = jnp.zeros((1, 128), F32)
    pieces = []
    for s, (row, filled) in enumerate(rows_of_slots(owner_ref, row_ref, me)):
        rows = pl.ds(pl.multiple_of(row * B, B), B)
        block = scaled_sum(g_ref[rows, :], o_ref[rows, :]).astype(BF16)
        half = jnp.dot(lroot_ref[s], block, preferred_element_type=F32).astype(BF16)
        prod = jnp.dot(half, rroot_ref[s], preferred_element_type=F32)
        square = jnp.sum(lanes_sum(prod * prod), axis=0, keepdims=True)
        psq_ref[s : s + 1, :] = square
        for _ in range(3):
            piece = square.astype(BF16)
            square = square - piece.astype(F32)
            pieces.append(piece.astype(F32))
        prod = prod.astype(BF16)
        for h in range(2):
            chunk = 2 * row + h
            home = jnp.where(chunk >= 3, jnp.int32(1), jnp.int32(0))
            place = pl.ds(pl.multiple_of((chunk - 3 * home) * HALF, HALF), HALF)
            piece = prod[h * HALF : (h + 1) * HALF]

            @pl.when((filled == 1) & (home == me))
            def _():
                mine_ref[place, :] = piece

            @pl.when((filled == 1) & (home != me))
            def _():
                send_ref[place, :] = piece
    tail = jnp.concatenate(pieces + [jnp.zeros((10, 128), F32)], axis=0).astype(BF16)
    send_ref[BLK * HALF :, :] = jnp.concatenate([tail] * 4, axis=1)


def products(owner, row_block, g, o, lroot, rroot, after):
    return pl.pallas_call(
        product_kernel,
        out_shape=(
            pltpu.VMEM((BLK * HALF, B), BF16),
            pltpu.VMEM((BLK * HALF + 16, B), BF16),
            pltpu.VMEM((CAP, 128), F32),
            pltpu.VMEM((1, 128), F32),
        ),
        in_specs=[SM, SM] + [VM] * 5,
        out_specs=(VM,) * 4,
        compiler_params=pltpu.CompilerParams(vmem_limit_bytes=12 * MIB),
        cost_estimate=pl.CostEstimate(
            flops=100 * B * B * B, bytes_accessed=8 * MIB, transcendentals=0
        ),
        name="products",
    )(owner, row_block, g, o, lroot, rroot, after)


NT = (((1,), (1,)), ((), ()))
TN = (((0,), (0,)), ((), ()))


def gram(x, y, dims):
    return lax.dot_general(x, y, dims, preferred_element_type=F32)


def gram_kernel(
    owner_ref, row_ref, g_ref, o_ref, moment_ref, other_ref, _,
    gl_ref, gr_ref, sq_ref, rs_ref, rold_ref, vec_ref, flag_ref, tick_ref, cross_ref,
):
    me = lax.axis_index("dp")
    tick_ref[...] = jnp.zeros((1, 128), F32)
    for b, (mine, slot) in enumerate(entry_of_blocks(owner_ref, row_ref, me)):
        rows = slice(b * B, (b + 1) * B)
        s = scaled_sum(g_ref[rows, :], o_ref[rows, :])
        s = s * s
        sq_ref[b] = s
        rs_ref[b] = jnp.broadcast_to(jnp.sum(lanes_sum(s), axis=1, keepdims=True), (B, 128))
        vec_ref[4 + b : 5 + b, :] = jnp.sum(s, axis=0, keepdims=True)
        own = mine == 1
        first = slot == 0
        rold = jnp.where(
            own,
            jnp.where(first, moment_ref[0:1, :], moment_ref[1:2, :]),
            jnp.where(first, other_ref[0:1, :], other_ref[1:2, :]),
        )
        rold_ref[b] = jnp.broadcast_to(rold, (128, B)).T
        vec_ref[8 + b : 9 + b, :] = jnp.where(
            own,
            jnp.where(first, moment_ref[2:3, :], moment_ref[3:4, :]),
            jnp.where(first, other_ref[2:3, :], other_ref[3:4, :]),
        )
        flag_ref[b : b + 1, :] = jnp.full((1, 128), mine, jnp.int32).astype(F32)
        flag_ref[4 + b : 5 + b, :] = jnp.full((1, 128), slot, jnp.int32).astype(F32)
    for s, (row, filled) in enumerate(rows_of_slots(owner_ref, row_ref, me)):
        flag_ref[8 + s : 9 + s, :] = jnp.full((1, 128), filled, jnp.int32).astype(F32)
        vec_ref[s : s + 1, :] = rs_ref[row].T[0:1, :]
        vec_ref[2 + s : 3 + s, :] = vec_ref[pl.ds(4 + row, 1), :]
        rows = pl.ds(pl.multiple_of(row * B, B), B)
        block = scaled_sum(g_ref[rows, :], o_ref[rows, :])
        hi = block.astype(BF16)
        lo = (block - hi.astype(F32)).astype(BF16)
        for out, dims in ((gl_ref, NT), (gr_ref, TN)):
            cross_ref[...] = gram(hi, lo, dims)
            out[s] = gram(hi, hi, dims)
            out[s] = out[s] + cross_ref[...] + cross_ref[...].T


def grams(owner, row_block, g, o, moments, others, after):
    return pl.pallas_call(
        gram_kernel,
        out_shape=(
            pltpu.VMEM((CAP, B, B), F32),
            pltpu.VMEM((CAP, B, B), F32),
            pltpu.VMEM((BLK, B, B), F32),
            pltpu.VMEM((BLK, B, 128), F32),
            pltpu.VMEM((BLK, B, 128), F32),
            pltpu.VMEM((16, B), F32),
            pltpu.VMEM((16, 128), F32),
            pltpu.VMEM((1, 128), F32),
        ),
        in_specs=[SM, SM] + [VM] * 5,
        out_specs=(VM,) * 8,
        scratch_shapes=[pltpu.VMEM((B, B), F32)],
        compiler_params=pltpu.CompilerParams(vmem_limit_bytes=12 * MIB),
        cost_estimate=pl.CostEstimate(
            flops=400 * B * B * B, bytes_accessed=12 * MIB, transcendentals=0
        ),
        name="grams",
    )(owner, row_block, g, o, moments, others, after)


def finish_kernel(
    total_ref, gl_ref, gr_ref, sq_ref, rs_ref, rold_ref, vec_ref, flag_ref,
    left_ref, right_ref, moment_ref, mine_ref, recv_ref, psq_ref,
    dir_hbm, nl_hbm, nr_hbm, nrows_hbm, ncols_hbm,
    nl_ref, nr_ref, dir_ref, nrows_ref, ncols_ref, sems, *, entries
):
    me = lax.axis_index("dp")
    total = jnp.sum(total_ref[...].reshape(-1, 128), axis=0, keepdims=True)
    total = jnp.sum(total, axis=1, keepdims=True)
    clip = lax.rsqrt(total * (1.0 / (SCALE * SCALE * entries)) + 1e-6) * (1.0 / SCALE)
    clip2 = clip * clip
    mix = (1.0 - DECAY) / B * clip2
    copies = []

    def send_out(src, dst, sem):
        copies.append(pltpu.make_async_copy(src, dst, sems.at[sem]))
        copies[-1].start()

    for s in range(CAP):
        filled = flag_ref[8 + s : 9 + s, 0:1]
        keep = 1.0 - (1.0 - DECAY) * filled
        add = mix * filled
        nrows_ref[s : s + 1, :] = keep * moment_ref[s : s + 1, :] + add * vec_ref[s : s + 1, :]
        ncols_ref[s : s + 1, :] = keep * moment_ref[2 + s : 3 + s, :] + add * vec_ref[2 + s : 3 + s, :]
        nl_ref[s] = keep * left_ref[s] + add * gl_ref[s]
        send_out(nl_ref.at[s], nl_hbm.at[s], 2 * s)
        nr_ref[s] = keep * right_ref[s] + add * gr_ref[s]
        send_out(nr_ref.at[s], nr_hbm.at[s], 2 * s + 1)
    send_out(nrows_ref, nrows_hbm, 4)
    send_out(ncols_ref, ncols_hbm, 5)
    factors, owns = [], []
    for i in range(2):
        b = me + i
        new_rows = DECAY * rold_ref[b] + mix * rs_ref[b]
        mean = jnp.sum(new_rows, axis=0, keepdims=True) * (1.0 / B)
        u = jnp.sqrt(new_rows / mean)
        v = jnp.sqrt(DECAY * vec_ref[pl.ds(8 + b, 1), :] + mix * vec_ref[pl.ds(4 + b, 1), :])
        acc = jnp.zeros((8, 128), F32)
        for j in range(4):
            cols = slice(128 * j, 128 * (j + 1))
            r = 1.0 / (u * v[:, cols] + 1e-8)
            acc = acc + jnp.sum((sq_ref[b, :, cols] * r * r).reshape(B // 8, 8, 128), axis=0)
        adam = jnp.sum(jnp.sum(acc, axis=0, keepdims=True), axis=1, keepdims=True)
        adam = adam * clip2 * (1.0 / (B * B))
        own = flag_ref[pl.ds(b, 1), :] > 0.5
        first = flag_ref[pl.ds(4 + b, 1), :] < 0.5
        tail = recv_ref[BLK * HALF :, 0:128].astype(F32)
        psq = jnp.where(
            own,
            jnp.where(first, psq_ref[0:1, :], psq_ref[1:2, :]),
            jnp.where(
                first,
                tail[0:1] + tail[1:2] + tail[2:3],
                tail[3:4] + tail[4:5] + tail[5:6],
            ),
        )
        psq = jnp.sum(psq, axis=1, keepdims=True) * clip2 * (1.0 / (B * B))
        factors.append(-clip * jnp.sqrt(adam) * lax.rsqrt(psq + 1e-6))
        owns.append(flag_ref[pl.ds(b, 1), 0:1])
    at_one = me == 1
    for j in range(BLK):
        rows = slice(j * HALF, (j + 1) * HALF)
        low, high = j // 2, (j + 1) // 2
        factor = jnp.where(at_one, factors[high], factors[low])
        own = jnp.where(at_one, owns[high], owns[low])
        piece = jnp.where(own > 0.5, mine_ref[rows, :].astype(F32), recv_ref[rows, :].astype(F32))
        dir_ref[rows, :] = (piece * factor).astype(BF16)
        send_out(dir_ref.at[rows, :], dir_hbm.at[rows, :], 6 + j)
    for c in copies:
        c.wait()


def finish(entries, *args):
    return pl.pallas_call(
        functools.partial(finish_kernel, entries=entries),
        out_shape=(
            jax.ShapeDtypeStruct((BLK * HALF, B), BF16),
            jax.ShapeDtypeStruct((CAP, B, B), F32),
            jax.ShapeDtypeStruct((CAP, B, B), F32),
            jax.ShapeDtypeStruct((CAP, B), F32),
            jax.ShapeDtypeStruct((CAP, B), F32),
        ),
        in_specs=[VM] * 14,
        out_specs=(HB,) * 5,
        scratch_shapes=[
            pltpu.VMEM((CAP, B, B), F32),
            pltpu.VMEM((CAP, B, B), F32),
            pltpu.VMEM((BLK * HALF, B), BF16),
            pltpu.VMEM((CAP, B), F32),
            pltpu.VMEM((CAP, B), F32),
            pltpu.SemaphoreType.DMA((9,)),
        ],
        compiler_params=pltpu.CompilerParams(vmem_limit_bytes=12 * MIB),
        cost_estimate=pl.CostEstimate(
            flops=16 * B * B, bytes_accessed=16 * MIB, transcendentals=0
        ),
        name="finish",
    )(*args)


def mp_swap(v, peer):
    pairs = []
    for z in range(8):
        for y in range(4):
            for x in range(4):
                to_z, to_y, to_x = peer(z, y, x)
                pairs.append(((z * 4 + y) * 4 + x, (to_z * 4 + to_y) * 4 + to_x))
    size = lax.axis_size("mp")
    return v + lax.ppermute(v, "mp", [p for p in pairs if max(p) < size])


def around(c, odd, size):
    return (((c + odd) ^ 1) - odd) % size


def swap_x(v, odd):
    return mp_swap(v, lambda z, y, x: (z, y, around(x, odd, 4)))


def rest_chips(v):
    if lax.axis_size("mp") != 128:
        return v
    groups = [[k * 4 + x for k in range(32)] for x in range(4)]
    many = jnp.broadcast_to(v, (32, 128))
    return lax.all_to_all(many, "mp", 0, 0, tiled=True, axis_index_groups=groups)


def on_device(
    grad_parts, owner, row_block, left_stats, right_stats, left_root, right_root, row_moment, col_moment
):
    entries = BLK * B * B * lax.axis_size("mp")
    o = lax.ppermute(grad_parts[0], "dp", SWAP)
    g, lroot, rroot, left, right, moments = load(
        grad_parts[0], left_root[0], right_root[0], left_stats[0], right_stats[0], row_moment[0], col_moment[0]
    )
    others = lax.ppermute(moments, "dp", SWAP)
    part = square_sum(g, o)
    mine, send, psq, tick = products(owner, row_block, g, o, lroot, rroot, part)
    recv = lax.ppermute(send, "dp", SWAP)
    part = swap_x(part, 0) + tick
    gl, gr, sq, rs, rold, vec, flag, tick = grams(owner, row_block, g, o, moments, others, part)
    total = rest_chips(swap_x(part, 1) + tick)
    direction, new_left, new_right, new_rows, new_cols = finish(
        entries, total, gl, gr, sq, rs, rold, vec, flag, left, right, moments, mine, recv, psq
    )
    return (direction, new_left[None], new_right[None], new_rows[None], new_cols[None])


def solution(mesh):
    return jax.shard_map(
        on_device,
        mesh=mesh,
        in_specs=(
            P("dp", None, "mp"),
            P("mp", None),
            P("mp", None),
            P("mp", "dp", None, None),
            P("mp", "dp", None, None),
            P("mp", "dp", None, None),
            P("mp", "dp", None, None),
            P("mp", "dp", None),
            P("mp", "dp", None),
        ),
        out_specs=(
            P("dp", "mp"),
            P("mp", "dp", None, None),
            P("mp", "dp", None, None),
            P("mp", "dp", None),
            P("mp", "dp", None),
        ),
        check_vma=False,
    )
```

```python
import functools

import jax
import jax.numpy as jnp
from jax import lax
from jax.experimental import pallas as pl
from jax.experimental.pallas import tpu as pltpu
from jax.sharding import PartitionSpec as P

DECAY = 0.95
SCALE = 1024.0
B = 512
BLK = 3
CAP = 2
HALF = B // 2
TAIL = 32
F32 = jnp.float32
BF16 = jnp.bfloat16
SWAP = [(0, 1), (1, 0)]
MIB = 1 << 20
VM = pl.BlockSpec(memory_space=pltpu.VMEM)
SM = pl.BlockSpec(memory_space=pltpu.SMEM)
HB = pl.BlockSpec(memory_space=pltpu.HBM)


def lanes_sum(x):
    return x[:, 0:128] + x[:, 128:256] + x[:, 256:384] + x[:, 384:512]


def scaled_sum(a, b):
    return (a.astype(F32) + b.astype(F32)) * SCALE


def square_kernel(g_ref, o_ref, out_ref):
    step = 64

    def body(i, acc):
        rows = pl.ds(pl.multiple_of(i * step, step), step)
        s = g_ref[rows, :].astype(F32) + o_ref[rows, :].astype(F32)
        s = s * s
        return acc + jnp.sum(s.reshape(step // 8, 8, B), axis=0)

    acc = lax.fori_loop(0, BLK * B // step, body, jnp.zeros((8, B), F32), unroll=4)
    out_ref[...] = jnp.sum(lanes_sum(acc), axis=0, keepdims=True)


def square_sum(g, o):
    return pl.pallas_call(
        square_kernel,
        out_shape=pltpu.VMEM((1, 128), F32),
        in_specs=[VM, VM],
        out_specs=VM,
        compiler_params=pltpu.CompilerParams(vmem_limit_bytes=8 * MIB),
        cost_estimate=pl.CostEstimate(
            flops=4 * BLK * B * B, bytes_accessed=4 * BLK * B * B, transcendentals=0
        ),
        name="squares",
    )(g, o)


def load_kernel(g_hbm, lroot_hbm, rroot_hbm, left_hbm, right_hbm, rows_hbm, cols_hbm,
                g_ref, lroot_ref, rroot_ref, left_ref, right_ref, moment_ref, rows_ref, cols_ref, sems):
    pairs = (
        (rows_hbm, rows_ref), (cols_hbm, cols_ref), (g_hbm, g_ref), (lroot_hbm, lroot_ref), (rroot_hbm, rroot_ref),
        (left_hbm, left_ref), (right_hbm, right_ref),
    )
    copies = [pltpu.make_async_copy(a, b, sems.at[i]) for i, (a, b) in enumerate(pairs)]
    for c in copies:
        c.start()
    for c in copies:
        c.wait()
    moment_ref[0:2, :] = rows_ref[...]
    moment_ref[2:4, :] = cols_ref[...]


def load(g, lroot, rroot, left, right, rows, cols):
    return pl.pallas_call(
        load_kernel,
        out_shape=(
            pltpu.VMEM((BLK * B, B), BF16),
            pltpu.VMEM((CAP, B, B), BF16),
            pltpu.VMEM((CAP, B, B), BF16),
            pltpu.VMEM((CAP, B, B), F32),
            pltpu.VMEM((CAP, B, B), F32),
            pltpu.VMEM((4, B), F32),
        ),
        in_specs=[HB] * 7,
        out_specs=(VM,) * 6,
        scratch_shapes=[
            pltpu.VMEM((CAP, B), F32),
            pltpu.VMEM((CAP, B), F32),
            pltpu.SemaphoreType.DMA((7,)),
        ],
        compiler_params=pltpu.CompilerParams(vmem_limit_bytes=2 * MIB),
        cost_estimate=pl.CostEstimate(flops=0, bytes_accessed=8 * MIB, transcendentals=0),
        name="load",
    )(*[pltpu.with_memory_space_constraint(a, pltpu.HBM) for a in (g, lroot, rroot, left, right, rows, cols)])


def slot_of_entry(owner_ref):
    o0, o1, o2 = owner_ref[0, 0], owner_ref[0, 1], owner_ref[0, 2]
    one = jnp.int32(1)
    zero = jnp.int32(0)
    s1 = jnp.where(o1 == o0, one, zero)
    s2 = jnp.where(o2 == o0, one, zero) + jnp.where(o2 == o1, one, zero)
    return (o0, o1, o2), (zero, s1, s2)


def rows_of_slots(owner_ref, row_ref, me):
    owners, slots = slot_of_entry(owner_ref)
    found = []
    for s in range(CAP):
        row, filled = jnp.int32(0), jnp.int32(0)
        for k in range(BLK):
            hit = (owners[k] == me) & (slots[k] == s)
            row = jnp.where(hit, row_ref[0, k], row)
            filled = jnp.where(hit, jnp.int32(1), filled)
        found.append((row, filled))
    return found


def entry_of_blocks(owner_ref, row_ref, me):
    owners, slots = slot_of_entry(owner_ref)
    found = []
    for b in range(BLK):
        mine, slot = jnp.int32(0), jnp.int32(0)
        for k in range(BLK):
            hit = row_ref[0, k] == b
            mine = jnp.where(hit & (owners[k] == me), jnp.int32(1), mine)
            slot = jnp.where(hit, slots[k], slot)
        found.append((mine, slot))
    return found


def thirds(x):
    parts = []
    for _ in range(3):
        part = x.astype(BF16).astype(F32)
        parts.append(part)
        x = x - part
    return parts


def product_kernel(
    owner_ref, row_ref, g_ref, o_ref, lroot_ref, rroot_ref, moment_ref, _,
    mine_ref, send_ref, psq_ref, hi_ref, lo_ref, sq_ref, rs_ref, colsum_ref, flag_ref, tick_ref, prod_ref,
):
    me = lax.axis_index("dp")
    tick_ref[...] = jnp.zeros((1, 128), F32)
    pieces = []
    for s, (row, filled) in enumerate(rows_of_slots(owner_ref, row_ref, me)):
        flag_ref[8 + s : 9 + s, :] = jnp.full((1, 128), filled, jnp.int32).astype(F32)
        rows = pl.ds(pl.multiple_of(row * B, B), B)
        block = scaled_sum(g_ref[rows, :], o_ref[rows, :])
        high = block.astype(BF16)
        hi_ref[s] = high
        lo_ref[s] = (block - high.astype(F32)).astype(BF16)
        half = jnp.dot(lroot_ref[s], high, preferred_element_type=F32).astype(BF16)
        prod = jnp.dot(half, rroot_ref[s], preferred_element_type=F32)
        prod_ref[s] = prod.astype(BF16)
        square = jnp.sum(lanes_sum(prod * prod), axis=0, keepdims=True)
        psq_ref[s : s + 1, :] = square
        pieces += thirds(jnp.concatenate([square] * 4, axis=1))
    own = entry_of_blocks(owner_ref, row_ref, me)
    at_one = me == 1
    for i in range(2):
        rows = pl.ds(pl.multiple_of((me + i) * B, B), B)
        s = scaled_sum(g_ref[rows, :], o_ref[rows, :])
        s = s * s
        sq_ref[i] = s
        rs_ref[i] = jnp.broadcast_to(jnp.sum(lanes_sum(s), axis=1, keepdims=True), (B, 128))
        colsum_ref[i : i + 1, :] = jnp.sum(s, axis=0, keepdims=True)
        for k in range(2):
            flag = jnp.where(at_one, own[i + 1][k], own[i][k])
            flag_ref[4 * k + i : 4 * k + i + 1, :] = jnp.full((1, 128), flag, jnp.int32).astype(F32)
    pieces += thirds(moment_ref[...]) + [jnp.zeros((TAIL - 18, B), F32)]
    send_ref[BLK * HALF :, :] = jnp.concatenate(pieces, axis=0).astype(BF16)
    for out, home in ((mine_ref, me), (send_ref, 1 - me)):
        for j in range(BLK):
            chunk = 3 * home + j
            block = lax.shift_right_logical(chunk, 1)
            slot = jnp.where(block == 0, own[0][1], jnp.where(block == 1, own[1][1], own[2][1]))
            rows = pl.ds(pl.multiple_of((chunk - 2 * block) * HALF, HALF), HALF)
            out[j * HALF : (j + 1) * HALF, :] = prod_ref[slot, rows, :]


def products(owner, row_block, g, o, lroot, rroot, moments, after):
    return pl.pallas_call(
        product_kernel,
        out_shape=(
            pltpu.VMEM((BLK * HALF, B), BF16),
            pltpu.VMEM((BLK * HALF + TAIL, B), BF16),
            pltpu.VMEM((CAP, 128), F32),
            pltpu.VMEM((CAP, B, B), BF16),
            pltpu.VMEM((CAP, B, B), BF16),
            pltpu.VMEM((2, B, B), F32),
            pltpu.VMEM((2, B, 128), F32),
            pltpu.VMEM((2, B), F32),
            pltpu.VMEM((16, 128), F32),
            pltpu.VMEM((1, 128), F32),
        ),
        in_specs=[SM, SM] + [VM] * 6,
        out_specs=(VM,) * 10,
        scratch_shapes=[pltpu.VMEM((CAP, B, B), BF16)],
        compiler_params=pltpu.CompilerParams(vmem_limit_bytes=12 * MIB),
        cost_estimate=pl.CostEstimate(
            flops=100 * B * B * B, bytes_accessed=8 * MIB, transcendentals=0
        ),
        name="products",
    )(owner, row_block, g, o, lroot, rroot, moments, after)


NT = (((1,), (1,)), ((), ()))
TN = (((0,), (0,)), ((), ()))


def gram(x, y, dims):
    return lax.dot_general(x, y, dims, preferred_element_type=F32)


def gram_kernel(
    hi_ref, lo_ref, _, gl_ref, gr_ref, vec_ref, tick_ref, cross_ref,
):
    tick_ref[...] = jnp.zeros((1, 128), F32)
    stats = ((gl_ref, NT), (gr_ref, TN))
    for s in range(CAP):
        hi, lo = hi_ref[s], lo_ref[s]
        for i, (out, dims) in enumerate(stats):
            cross_ref[2 * s + i] = gram(hi, lo, dims)
            out[s] = gram(hi, hi, dims)
    diagonal = lax.broadcasted_iota(jnp.int32, (128, 128), 0) == lax.broadcasted_iota(
        jnp.int32, (128, 128), 1
    )
    for s in range(CAP):
        for i, (out, _) in enumerate(stats):
            out[s] = out[s] + cross_ref[2 * s + i] + cross_ref[2 * s + i].T
            for p in range(4):
                at = slice(128 * p, 128 * (p + 1))
                line = jnp.where(diagonal, out[s, at, at], 0.0)
                vec_ref[2 * i + s : 2 * i + s + 1, at] = jnp.sum(line, axis=0, keepdims=True)


def grams(hi, lo, after):
    return pl.pallas_call(
        gram_kernel,
        out_shape=(
            pltpu.VMEM((CAP, B, B), F32),
            pltpu.VMEM((CAP, B, B), F32),
            pltpu.VMEM((4, B), F32),
            pltpu.VMEM((1, 128), F32),
        ),
        in_specs=[VM] * 3,
        out_specs=(VM,) * 4,
        scratch_shapes=[pltpu.VMEM((2 * CAP, B, B), F32)],
        compiler_params=pltpu.CompilerParams(vmem_limit_bytes=12 * MIB),
        cost_estimate=pl.CostEstimate(
            flops=400 * B * B * B, bytes_accessed=12 * MIB, transcendentals=0
        ),
        name="grams",
    )(hi, lo, after)


def finish_kernel(
    total_ref, gl_ref, gr_ref, sq_ref, rs_ref, colsum_ref, vec_ref, flag_ref,
    left_ref, right_ref, moment_ref, mine_ref, recv_ref, psq_ref,
    dir_hbm, nl_hbm, nr_hbm, nrows_hbm, ncols_hbm,
    nl_ref, nr_ref, dir_ref, nrows_ref, ncols_ref, sems, *, entries
):
    me = lax.axis_index("dp")
    total = jnp.sum(total_ref[...].reshape(-1, 128), axis=0, keepdims=True)
    total = jnp.sum(total, axis=1, keepdims=True)
    clip = lax.rsqrt(total * (1.0 / entries) + 1e-6) * (1.0 / SCALE)
    clip2 = clip * clip
    mix = (1.0 - DECAY) / B * clip2
    copies = []

    def send_out(src, dst, sem):
        copies.append(pltpu.make_async_copy(src, dst, sems.at[sem]))
        copies[-1].start()

    for s in range(CAP):
        filled = flag_ref[8 + s : 9 + s, 0:1]
        keep = 1.0 - (1.0 - DECAY) * filled
        add = mix * filled
        nrows_ref[s : s + 1, :] = keep * moment_ref[s : s + 1, :] + add * vec_ref[s : s + 1, :]
        ncols_ref[s : s + 1, :] = keep * moment_ref[2 + s : 3 + s, :] + add * vec_ref[2 + s : 3 + s, :]
        for i, (new, old, stat, hbm) in enumerate(
            ((nl_ref, left_ref, gl_ref, nl_hbm), (nr_ref, right_ref, gr_ref, nr_hbm))
        ):
            for h in range(4):
                rows = slice(h * 128, (h + 1) * 128)
                new[s, rows, :] = keep * old[s, rows, :] + add * stat[s, rows, :]
                send_out(new.at[s, rows, :], hbm.at[s, rows, :], 8 * s + 4 * i + h)
    send_out(nrows_ref, nrows_hbm, 16)
    send_out(ncols_ref, ncols_hbm, 17)
    factors, owns = [], []
    tail = recv_ref[BLK * HALF :, :].astype(F32)
    others = tail[6:10] + tail[10:14] + tail[14:18]
    for i in range(2):
        own = flag_ref[i : i + 1, 0:1] > 0.5
        first = flag_ref[4 + i : 5 + i, 0:1] < 0.5

        def pick(mine, theirs, k):
            return jnp.where(
                own,
                jnp.where(first, mine[k : k + 1, :], mine[k + 1 : k + 2, :]),
                jnp.where(first, theirs[k : k + 1, :], theirs[k + 1 : k + 2, :]),
            )

        old_rows = jnp.broadcast_to(pick(moment_ref, others, 0), (128, B)).T
        new_rows = DECAY * old_rows + mix * rs_ref[i]
        mean = jnp.sum(new_rows, axis=0, keepdims=True) * (1.0 / B)
        share = new_rows * (1.0 / mean)
        u = share * lax.rsqrt(share)
        v = jnp.sqrt(DECAY * pick(moment_ref, others, 2) + mix * colsum_ref[i : i + 1, :])
        acc = jnp.zeros((8, 128), F32)
        for j in range(4):
            cols = slice(128 * j, 128 * (j + 1))
            r = pl.reciprocal(u * v[:, cols] + 1e-8, approx=True)
            acc = acc + jnp.sum((sq_ref[i, :, cols] * r * r).reshape(B // 8, 8, 128), axis=0)
        adam = jnp.sum(jnp.sum(acc, axis=0, keepdims=True), axis=1, keepdims=True)
        adam = adam * clip2 * (1.0 / (B * B))
        theirs = jnp.concatenate(
            [tail[0:1] + tail[1:2] + tail[2:3], tail[3:4] + tail[4:5] + tail[5:6]], axis=0
        )
        psq = pick(psq_ref, theirs[:, 0:128], 0)
        psq = jnp.sum(psq, axis=1, keepdims=True) * clip2 * (1.0 / (B * B))
        factors.append(-clip * jnp.sqrt(adam) * lax.rsqrt(psq + 1e-6))
        owns.append(flag_ref[i : i + 1, 0:1])
    at_one = me == 1
    for j in range(BLK):
        rows = slice(j * HALF, (j + 1) * HALF)
        low, high = j // 2, (j + 1) // 2
        factor = jnp.where(at_one, factors[high], factors[low])
        own = jnp.where(at_one, owns[high], owns[low])
        piece = jnp.where(own > 0.5, mine_ref[rows, :].astype(F32), recv_ref[rows, :].astype(F32))
        dir_ref[rows, :] = (piece * factor).astype(BF16)
        send_out(dir_ref.at[rows, :], dir_hbm.at[rows, :], 18 + j)
    for c in copies:
        c.wait()


def finish(entries, *args):
    return pl.pallas_call(
        functools.partial(finish_kernel, entries=entries),
        out_shape=(
            jax.ShapeDtypeStruct((BLK * HALF, B), BF16),
            jax.ShapeDtypeStruct((CAP, B, B), F32),
            jax.ShapeDtypeStruct((CAP, B, B), F32),
            jax.ShapeDtypeStruct((CAP, B), F32),
            jax.ShapeDtypeStruct((CAP, B), F32),
        ),
        in_specs=[VM] * 14,
        out_specs=(HB,) * 5,
        scratch_shapes=[
            pltpu.VMEM((CAP, B, B), F32),
            pltpu.VMEM((CAP, B, B), F32),
            pltpu.VMEM((BLK * HALF, B), BF16),
            pltpu.VMEM((CAP, B), F32),
            pltpu.VMEM((CAP, B), F32),
            pltpu.SemaphoreType.DMA((21,)),
        ],
        compiler_params=pltpu.CompilerParams(vmem_limit_bytes=12 * MIB),
        cost_estimate=pl.CostEstimate(
            flops=16 * B * B, bytes_accessed=16 * MIB, transcendentals=0
        ),
        name="finish",
    )(*args)


def around(c, odd, size):
    return (((c + odd) ^ 1) - odd) % size


ROUNDS = (
    lambda z, y, x: (z, y, around(x, 0, 4)),
    lambda z, y, x: (z, y, around(x, 1, 4)),
)


def chip(z, y, x):
    return (z * 4 + y) * 4 + x


def mp_swap(v, peer):
    size = lax.axis_size("mp")
    pairs = [
        (chip(z, y, x), chip(*peer(z, y, x)))
        for z in range(8) for y in range(4) for x in range(4)
    ]
    return v + lax.ppermute(v, "mp", [p for p in pairs if max(p) < size])


def rest_chips(v):
    if lax.axis_size("mp") != 128:
        return v
    groups = [[chip(z, y, x) for z in range(8) for y in range(4)] for x in range(4)]
    many = jnp.broadcast_to(v, (len(groups[0]), 128))
    return lax.all_to_all(many, "mp", 0, 0, tiled=True, axis_index_groups=groups)


def on_device(
    grad_parts, owner, row_block, left_stats, right_stats, left_root, right_root, row_moment, col_moment
):
    entries = BLK * B * B * lax.axis_size("mp")
    o = lax.ppermute(grad_parts[0], "dp", SWAP)
    g, lroot, rroot, left, right, moments = load(
        grad_parts[0], left_root[0], right_root[0], left_stats[0], right_stats[0], row_moment[0], col_moment[0]
    )
    part = square_sum(g, o)
    mine, send, psq, hi, lo, sq, rs, colsum, flag, tick = products(owner, row_block, g, o, lroot, rroot, moments, part)
    recv = lax.ppermute(send, "dp", SWAP)
    part = mp_swap(part, ROUNDS[0]) + tick
    gl, gr, vec, tick = grams(hi, lo, part)
    part = mp_swap(part, ROUNDS[1]) + tick
    total = rest_chips(part)
    direction, new_left, new_right, new_rows, new_cols = finish(
        entries, total, gl, gr, sq, rs, colsum, vec, flag, left, right, moments, mine, recv, psq
    )
    return (direction, new_left[None], new_right[None], new_rows[None], new_cols[None])


def solution(mesh):
    return jax.shard_map(
        on_device,
        mesh=mesh,
        in_specs=(
            P("dp", None, "mp"),
            P("mp", None),
            P("mp", None),
            P("mp", "dp", None, None),
            P("mp", "dp", None, None),
            P("mp", "dp", None, None),
            P("mp", "dp", None, None),
            P("mp", "dp", None),
            P("mp", "dp", None),
        ),
        out_specs=(
            P("dp", "mp"),
            P("mp", "dp", None, None),
            P("mp", "dp", None, None),
            P("mp", "dp", None),
            P("mp", "dp", None),
        ),
        check_vma=False,
    )
```

```python
import functools

import jax
import jax.numpy as jnp
from jax import lax
from jax.experimental import pallas as pl
from jax.experimental.pallas import tpu as pltpu
from jax.sharding import PartitionSpec as P

DECAY = 0.95
SCALE = 1024.0
B = 512
BLK = 3
CAP = 2
HALF = B // 2
TAIL = 32
F32 = jnp.float32
BF16 = jnp.bfloat16
SWAP = [(0, 1), (1, 0)]
MIB = 1 << 20
VM = pl.BlockSpec(memory_space=pltpu.VMEM)
SM = pl.BlockSpec(memory_space=pltpu.SMEM)
HB = pl.BlockSpec(memory_space=pltpu.HBM)


def lanes_sum(x):
    return x[:, 0:128] + x[:, 128:256] + x[:, 256:384] + x[:, 384:512]


def scaled_sum(a, b):
    return (a.astype(F32) + b.astype(F32)) * SCALE


def square_kernel(g_ref, o_ref, out_ref):
    step = 64

    def body(i, acc):
        rows = pl.ds(pl.multiple_of(i * step, step), step)
        s = g_ref[rows, :].astype(F32) + o_ref[rows, :].astype(F32)
        s = s * s
        return acc + jnp.sum(s.reshape(step // 8, 8, B), axis=0)

    acc = lax.fori_loop(0, BLK * B // step, body, jnp.zeros((8, B), F32), unroll=4)
    out_ref[...] = jnp.sum(lanes_sum(acc), axis=0, keepdims=True)


def square_sum(g, o):
    return pl.pallas_call(
        square_kernel,
        out_shape=pltpu.VMEM((1, 128), F32),
        in_specs=[VM, VM],
        out_specs=VM,
        compiler_params=pltpu.CompilerParams(vmem_limit_bytes=8 * MIB),
        cost_estimate=pl.CostEstimate(
            flops=4 * BLK * B * B, bytes_accessed=4 * BLK * B * B, transcendentals=0
        ),
        name="squares",
    )(g, o)


def load_kernel(g_hbm, lroot_hbm, rroot_hbm, left_hbm, right_hbm, rows_hbm, cols_hbm,
                g_ref, lroot_ref, rroot_ref, left_ref, right_ref, moment_ref, part_ref, rows_ref, cols_ref, sems):
    pairs = [
        (g_hbm, part_ref), (rows_hbm, rows_ref), (cols_hbm, cols_ref),
        (left_hbm.at[0], left_ref.at[0]), (right_hbm.at[0], right_ref.at[0]),
        (lroot_hbm, lroot_ref), (rroot_hbm, rroot_ref),
        (left_hbm.at[1], left_ref.at[1]), (right_hbm.at[1], right_ref.at[1]),
    ]
    copies = [pltpu.make_async_copy(a, b, sems.at[i]) for i, (a, b) in enumerate(pairs)]
    for c in copies:
        c.start()
    copies[0].wait()
    step = 64

    def widen(i, carry):
        rows = pl.ds(pl.multiple_of(i * step, step), step)
        g_ref[rows, :] = part_ref[rows, :].astype(F32)
        return carry

    lax.fori_loop(0, BLK * B // step, widen, 0, unroll=4)
    for c in copies[1:5]:
        c.wait()
    moment_ref[0:2, :] = rows_ref[...]
    moment_ref[2:4, :] = cols_ref[...]
    left_ref[0] = left_ref[0] * DECAY
    right_ref[0] = right_ref[0] * DECAY
    for c in copies[5:]:
        c.wait()


def in_hbm(*arrays):
    return [pltpu.with_memory_space_constraint(a, pltpu.HBM) for a in arrays]


def load(g, lroot, rroot, left, right, rows, cols):
    return pl.pallas_call(
        load_kernel,
        out_shape=(
            pltpu.VMEM((BLK * B, B), F32),
            pltpu.VMEM((CAP, B, B), BF16),
            pltpu.VMEM((CAP, B, B), BF16),
            pltpu.VMEM((CAP, B, B), F32),
            pltpu.VMEM((CAP, B, B), F32),
            pltpu.VMEM((4, B), F32),
        ),
        in_specs=[HB] * 7,
        out_specs=(VM,) * 6,
        scratch_shapes=[
            pltpu.VMEM((BLK * B, B), BF16),
            pltpu.VMEM((CAP, B), F32),
            pltpu.VMEM((CAP, B), F32),
            pltpu.SemaphoreType.DMA((9,)),
        ],
        compiler_params=pltpu.CompilerParams(vmem_limit_bytes=4 * MIB),
        cost_estimate=pl.CostEstimate(flops=0, bytes_accessed=8 * MIB, transcendentals=0),
        name="load",
    )(*in_hbm(g, lroot, rroot, left, right, rows, cols))


def slot_of_entry(owner_ref):
    o0, o1, o2 = owner_ref[0, 0], owner_ref[0, 1], owner_ref[0, 2]
    one = jnp.int32(1)
    zero = jnp.int32(0)
    s1 = jnp.where(o1 == o0, one, zero)
    s2 = jnp.where(o2 == o0, one, zero) + jnp.where(o2 == o1, one, zero)
    return (o0, o1, o2), (zero, s1, s2)


def rows_of_slots(owner_ref, row_ref, me):
    owners, slots = slot_of_entry(owner_ref)
    found = []
    for s in range(CAP):
        row, filled = jnp.int32(0), jnp.int32(0)
        for k in range(BLK):
            hit = (owners[k] == me) & (slots[k] == s)
            row = jnp.where(hit, row_ref[0, k], row)
            filled = jnp.where(hit, jnp.int32(1), filled)
        found.append((row, filled))
    return found


def entry_of_blocks(owner_ref, row_ref, me):
    owners, slots = slot_of_entry(owner_ref)
    found = []
    for b in range(BLK):
        mine, slot = jnp.int32(0), jnp.int32(0)
        for k in range(BLK):
            hit = row_ref[0, k] == b
            mine = jnp.where(hit & (owners[k] == me), jnp.int32(1), mine)
            slot = jnp.where(hit, slots[k], slot)
        found.append((mine, slot))
    return found


def thirds(x):
    parts = []
    for _ in range(3):
        part = x.astype(BF16).astype(F32)
        parts.append(part)
        x = x - part
    return parts


def product_kernel(
    owner_ref, row_ref, g_ref, o_ref, lroot_ref, rroot_ref, moment_ref, _,
    mine_ref, send_ref, psq_ref, hi_ref, lo_ref, sq_ref, rs_ref, colsum_ref, flag_ref, tick_ref, prod_ref,
):
    me = lax.axis_index("dp")
    tick_ref[...] = jnp.zeros((1, 128), F32)
    pieces = []
    for s, (row, filled) in enumerate(rows_of_slots(owner_ref, row_ref, me)):
        flag_ref[8 + s : 9 + s, :] = jnp.full((1, 128), filled, jnp.int32).astype(F32)
        rows = pl.ds(pl.multiple_of(row * B, B), B)
        block = scaled_sum(g_ref[rows, :], o_ref[rows, :])
        high = block.astype(BF16)
        hi_ref[s] = high
        lo_ref[s] = (block - high.astype(F32)).astype(BF16)
        half = jnp.dot(lroot_ref[s], high, preferred_element_type=F32).astype(BF16)
        prod = jnp.dot(half, rroot_ref[s], preferred_element_type=F32)
        prod_ref[s] = prod.astype(BF16)
        square = jnp.sum(lanes_sum(prod * prod), axis=0, keepdims=True)
        psq_ref[s : s + 1, :] = square
        pieces += thirds(jnp.concatenate([square] * 4, axis=1))
    own = entry_of_blocks(owner_ref, row_ref, me)
    at_one = me == 1
    for i in range(2):
        rows = pl.ds(pl.multiple_of((me + i) * B, B), B)
        s = scaled_sum(g_ref[rows, :], o_ref[rows, :])
        s = s * s
        sq_ref[i] = s
        rs_ref[i] = jnp.broadcast_to(jnp.sum(lanes_sum(s), axis=1, keepdims=True), (B, 128))
        colsum_ref[i : i + 1, :] = jnp.sum(s, axis=0, keepdims=True)
        for k in range(2):
            flag = jnp.where(at_one, own[i + 1][k], own[i][k])
            flag_ref[4 * k + i : 4 * k + i + 1, :] = jnp.full((1, 128), flag, jnp.int32).astype(F32)
    pieces += thirds(moment_ref[...]) + [jnp.zeros((TAIL - 18, B), F32)]
    send_ref[BLK * HALF :, :] = jnp.concatenate(pieces, axis=0).astype(BF16)
    for out, home in ((mine_ref, me), (send_ref, 1 - me)):
        for j in range(BLK):
            chunk = 3 * home + j
            block = lax.shift_right_logical(chunk, 1)
            slot = jnp.where(block == 0, own[0][1], jnp.where(block == 1, own[1][1], own[2][1]))
            rows = pl.ds(pl.multiple_of((chunk - 2 * block) * HALF, HALF), HALF)
            out[j * HALF : (j + 1) * HALF, :] = prod_ref[slot, rows, :]


def products(owner, row_block, g, o, lroot, rroot, moments, after):
    return pl.pallas_call(
        product_kernel,
        out_shape=(
            pltpu.VMEM((BLK * HALF, B), BF16),
            pltpu.VMEM((BLK * HALF + TAIL, B), BF16),
            pltpu.VMEM((CAP, 128), F32),
            pltpu.VMEM((CAP, B, B), BF16),
            pltpu.VMEM((CAP, B, B), BF16),
            pltpu.VMEM((2, B, B), F32),
            pltpu.VMEM((2, B, 128), F32),
            pltpu.VMEM((2, B), F32),
            pltpu.VMEM((16, 128), F32),
            pltpu.VMEM((1, 128), F32),
        ),
        in_specs=[SM, SM] + [VM] * 6,
        out_specs=(VM,) * 10,
        scratch_shapes=[pltpu.VMEM((CAP, B, B), BF16)],
        compiler_params=pltpu.CompilerParams(vmem_limit_bytes=12 * MIB),
        cost_estimate=pl.CostEstimate(
            flops=100 * B * B * B, bytes_accessed=8 * MIB, transcendentals=0
        ),
        name="products",
    )(owner, row_block, g, o, lroot, rroot, moments, after)


NT = (((1,), (1,)), ((), ()))
TN = (((0,), (0,)), ((), ()))


def gram(x, y, dims):
    return lax.dot_general(x, y, dims, preferred_element_type=F32)


def gram_kernel(
    hi_ref, lo_ref, _, gl_ref, gr_ref, vec_ref, tick_ref, cross_ref,
):
    tick_ref[...] = jnp.zeros((1, 128), F32)
    stats = ((gl_ref, NT), (gr_ref, TN))
    for s in range(CAP):
        hi, lo = hi_ref[s], lo_ref[s]
        for i, (out, dims) in enumerate(stats):
            cross_ref[2 * s + i] = gram(hi, lo, dims)
            out[s] = gram(hi, hi, dims)
    diagonal = lax.broadcasted_iota(jnp.int32, (128, 128), 0) == lax.broadcasted_iota(
        jnp.int32, (128, 128), 1
    )
    for s in range(CAP):
        for i, (out, _) in enumerate(stats):
            out[s] = out[s] + cross_ref[2 * s + i] + cross_ref[2 * s + i].T
            for p in range(4):
                at = slice(128 * p, 128 * (p + 1))
                line = jnp.where(diagonal, out[s, at, at], 0.0)
                vec_ref[2 * i + s : 2 * i + s + 1, at] = jnp.sum(line, axis=0, keepdims=True)


def grams(hi, lo, after):
    return pl.pallas_call(
        gram_kernel,
        out_shape=(
            pltpu.VMEM((CAP, B, B), F32),
            pltpu.VMEM((CAP, B, B), F32),
            pltpu.VMEM((4, B), F32),
            pltpu.VMEM((1, 128), F32),
        ),
        in_specs=[VM] * 3,
        out_specs=(VM,) * 4,
        scratch_shapes=[pltpu.VMEM((2 * CAP, B, B), F32)],
        compiler_params=pltpu.CompilerParams(vmem_limit_bytes=12 * MIB),
        cost_estimate=pl.CostEstimate(
            flops=400 * B * B * B, bytes_accessed=12 * MIB, transcendentals=0
        ),
        name="grams",
    )(hi, lo, after)


def finish_kernel(
    total_ref, gl_ref, gr_ref, sq_ref, rs_ref, colsum_ref, vec_ref, flag_ref,
    left_ref, right_ref, moment_ref, mine_ref, recv_ref, psq_ref,
    dir_hbm, nl_hbm, nr_hbm, nrows_hbm, ncols_hbm,
    nl_ref, nr_ref, dir_ref, nrows_ref, ncols_ref, sems, *, entries
):
    me = lax.axis_index("dp")
    total = jnp.sum(total_ref[...].reshape(-1, 128), axis=0, keepdims=True)
    total = jnp.sum(total, axis=1, keepdims=True)
    clip = lax.rsqrt(total * (1.0 / entries) + 1e-6) * (1.0 / SCALE)
    clip2 = clip * clip
    mix = (1.0 - DECAY) / B * clip2
    copies = []

    def send_out(src, dst, sem):
        copies.append(pltpu.make_async_copy(src, dst, sems.at[sem]))
        copies[-1].start()

    for s in range(CAP):
        filled = flag_ref[8 + s : 9 + s, 0:1]
        keep = 1.0 - (1.0 - DECAY) * filled
        add = mix * filled
        nrows_ref[s : s + 1, :] = keep * moment_ref[s : s + 1, :] + add * vec_ref[s : s + 1, :]
        ncols_ref[s : s + 1, :] = keep * moment_ref[2 + s : 3 + s, :] + add * vec_ref[2 + s : 3 + s, :]
        for i, (new, old, stat, hbm) in enumerate(
            ((nl_ref, left_ref, gl_ref, nl_hbm), (nr_ref, right_ref, gr_ref, nr_hbm))
        ):
            for h in range(4):
                rows = slice(h * 128, (h + 1) * 128)
                kept = old[s, rows, :] if s == 0 else keep * old[s, rows, :]
                new[s, rows, :] = kept + add * stat[s, rows, :]
                send_out(new.at[s, rows, :], hbm.at[s, rows, :], 8 * s + 4 * i + h)
    send_out(nrows_ref, nrows_hbm, 16)
    send_out(ncols_ref, ncols_hbm, 17)
    factors, owns = [], []
    tail = recv_ref[BLK * HALF :, :].astype(F32)
    others = tail[6:10] + tail[10:14] + tail[14:18]
    for i in range(2):
        own = flag_ref[i : i + 1, 0:1] > 0.5
        first = flag_ref[4 + i : 5 + i, 0:1] < 0.5

        def pick(mine, theirs, k):
            return jnp.where(
                own,
                jnp.where(first, mine[k : k + 1, :], mine[k + 1 : k + 2, :]),
                jnp.where(first, theirs[k : k + 1, :], theirs[k + 1 : k + 2, :]),
            )

        old_rows = jnp.broadcast_to(pick(moment_ref, others, 0), (128, B)).T
        new_rows = DECAY * old_rows + mix * rs_ref[i]
        mean = jnp.sum(new_rows, axis=0, keepdims=True) * (1.0 / B)
        share = new_rows * (1.0 / mean)
        u = share * lax.rsqrt(share)
        v = jnp.sqrt(DECAY * pick(moment_ref, others, 2) + mix * colsum_ref[i : i + 1, :])
        acc = jnp.zeros((8, 128), F32)
        for j in range(4):
            cols = slice(128 * j, 128 * (j + 1))
            r = pl.reciprocal(u * v[:, cols] + 1e-8, approx=True)
            acc = acc + jnp.sum((sq_ref[i, :, cols] * r * r).reshape(B // 8, 8, 128), axis=0)
        adam = jnp.sum(jnp.sum(acc, axis=0, keepdims=True), axis=1, keepdims=True)
        adam = adam * clip2 * (1.0 / (B * B))
        theirs = jnp.concatenate(
            [tail[0:1] + tail[1:2] + tail[2:3], tail[3:4] + tail[4:5] + tail[5:6]], axis=0
        )
        psq = pick(psq_ref, theirs[:, 0:128], 0)
        psq = jnp.sum(psq, axis=1, keepdims=True) * clip2 * (1.0 / (B * B))
        factors.append(-clip * jnp.sqrt(adam) * lax.rsqrt(psq + 1e-6))
        owns.append(flag_ref[i : i + 1, 0:1])
    at_one = me == 1
    for j in range(BLK):
        rows = slice(j * HALF, (j + 1) * HALF)
        low, high = j // 2, (j + 1) // 2
        factor = jnp.where(at_one, factors[high], factors[low])
        own = jnp.where(at_one, owns[high], owns[low])
        piece = jnp.where(own > 0.5, mine_ref[rows, :].astype(F32), recv_ref[rows, :].astype(F32))
        dir_ref[rows, :] = (piece * factor).astype(BF16)
        send_out(dir_ref.at[rows, :], dir_hbm.at[rows, :], 18 + j)
    for c in copies:
        c.wait()


def finish(entries, *args):
    return pl.pallas_call(
        functools.partial(finish_kernel, entries=entries),
        out_shape=(
            jax.ShapeDtypeStruct((BLK * HALF, B), BF16),
            jax.ShapeDtypeStruct((CAP, B, B), F32),
            jax.ShapeDtypeStruct((CAP, B, B), F32),
            jax.ShapeDtypeStruct((CAP, B), F32),
            jax.ShapeDtypeStruct((CAP, B), F32),
        ),
        in_specs=[VM] * 14,
        out_specs=(HB,) * 5,
        scratch_shapes=[
            pltpu.VMEM((CAP, B, B), F32),
            pltpu.VMEM((CAP, B, B), F32),
            pltpu.VMEM((BLK * HALF, B), BF16),
            pltpu.VMEM((CAP, B), F32),
            pltpu.VMEM((CAP, B), F32),
            pltpu.SemaphoreType.DMA((21,)),
        ],
        compiler_params=pltpu.CompilerParams(vmem_limit_bytes=12 * MIB),
        cost_estimate=pl.CostEstimate(
            flops=16 * B * B, bytes_accessed=16 * MIB, transcendentals=0
        ),
        name="finish",
    )(*args)


def around(c, odd, size):
    return (((c + odd) ^ 1) - odd) % size


ROUNDS = (
    lambda z, y, x: (z, y, around(x, 0, 4)),
    lambda z, y, x: (z, y, around(x, 1, 4)),
)


def chip(z, y, x):
    return (z * 4 + y) * 4 + x


def mp_swap(v, peer):
    size = lax.axis_size("mp")
    pairs = [
        (chip(z, y, x), chip(*peer(z, y, x)))
        for z in range(8) for y in range(4) for x in range(4)
    ]
    return v + lax.ppermute(v, "mp", [p for p in pairs if max(p) < size])


def rest_chips(v):
    if lax.axis_size("mp") != 128:
        return v
    groups = [[chip(z, y, x) for z in range(8) for y in range(4)] for x in range(4)]
    many = jnp.broadcast_to(v, (len(groups[0]), 128))
    return lax.all_to_all(many, "mp", 0, 0, tiled=True, axis_index_groups=groups)


def on_device(
    grad_parts, owner, row_block, left_stats, right_stats, left_root, right_root, row_moment, col_moment
):
    entries = BLK * B * B * lax.axis_size("mp")
    o = lax.ppermute(grad_parts[0], "dp", SWAP)
    g, lroot, rroot, left, right, moments = load(
        grad_parts[0], left_root[0], right_root[0], left_stats[0], right_stats[0], row_moment[0], col_moment[0]
    )
    part = square_sum(g, o)
    mine, send, psq, hi, lo, sq, rs, colsum, flag, tick = products(owner, row_block, g, o, lroot, rroot, moments, part)
    recv = lax.ppermute(send, "dp", SWAP)
    part = mp_swap(part, ROUNDS[0]) + tick
    gl, gr, vec, tick = grams(hi, lo, part)
    part = mp_swap(part, ROUNDS[1]) + tick
    total = rest_chips(part)
    direction, new_left, new_right, new_rows, new_cols = finish(
        entries, total, gl, gr, sq, rs, colsum, vec, flag, left, right, moments, mine, recv, psq
    )
    return (direction, new_left[None], new_right[None], new_rows[None], new_cols[None])


def solution(mesh):
    return jax.shard_map(
        on_device,
        mesh=mesh,
        in_specs=(
            P("dp", None, "mp"),
            P("mp", None),
            P("mp", None),
            P("mp", "dp", None, None),
            P("mp", "dp", None, None),
            P("mp", "dp", None, None),
            P("mp", "dp", None, None),
            P("mp", "dp", None),
            P("mp", "dp", None),
        ),
        out_specs=(
            P("dp", "mp"),
            P("mp", "dp", None, None),
            P("mp", "dp", None, None),
            P("mp", "dp", None),
            P("mp", "dp", None),
        ),
        check_vma=False,
    )
```

```python
import functools

import jax
import jax.numpy as jnp
from jax import lax
from jax.experimental import pallas as pl
from jax.experimental.pallas import tpu as pltpu
from jax.sharding import PartitionSpec as P

DECAY = 0.95
SCALE = 1024.0
B = 512
BLK = 3
CAP = 2
HALF = B // 2
TAIL = 32
F32 = jnp.float32
BF16 = jnp.bfloat16
SWAP = [(0, 1), (1, 0)]
MIB = 1 << 20
VM = pl.BlockSpec(memory_space=pltpu.VMEM)
SM = pl.BlockSpec(memory_space=pltpu.SMEM)
HB = pl.BlockSpec(memory_space=pltpu.HBM)


def lanes_sum(x):
    return x[:, 0:128] + x[:, 128:256] + x[:, 256:384] + x[:, 384:512]


def scaled_sum(a, b):
    return (a.astype(F32) + b.astype(F32)) * SCALE


def square_kernel(g_ref, o_ref, out_ref):
    step = 64

    def body(i, acc):
        rows = pl.ds(pl.multiple_of(i * step, step), step)
        s = g_ref[rows, :].astype(F32) + o_ref[rows, :].astype(F32)
        s = s * s
        return acc + jnp.sum(s.reshape(step // 8, 8, B), axis=0)

    acc = lax.fori_loop(0, BLK * B // step, body, jnp.zeros((8, B), F32), unroll=4)
    out_ref[...] = jnp.sum(lanes_sum(acc), axis=0, keepdims=True)


def square_sum(g, o):
    return pl.pallas_call(
        square_kernel,
        out_shape=pltpu.VMEM((1, 128), F32),
        in_specs=[VM, VM],
        out_specs=VM,
        compiler_params=pltpu.CompilerParams(vmem_limit_bytes=8 * MIB),
        cost_estimate=pl.CostEstimate(
            flops=4 * BLK * B * B, bytes_accessed=4 * BLK * B * B, transcendentals=0
        ),
        name="squares",
    )(g, o)


def load_kernel(g_hbm, lroot_hbm, rroot_hbm, left_hbm, right_hbm, rows_hbm, cols_hbm,
                g_ref, lroot_ref, rroot_ref, left_ref, right_ref, moment_ref, part_ref, rows_ref, cols_ref, sems):
    pairs = [
        (g_hbm, part_ref), (rows_hbm, rows_ref), (cols_hbm, cols_ref),
        (left_hbm.at[0], left_ref.at[0]), (right_hbm.at[0], right_ref.at[0]),
        (lroot_hbm, lroot_ref), (rroot_hbm, rroot_ref),
        (left_hbm.at[1], left_ref.at[1]), (right_hbm.at[1], right_ref.at[1]),
    ]
    copies = [pltpu.make_async_copy(a, b, sems.at[i]) for i, (a, b) in enumerate(pairs)]
    for c in copies:
        c.start()
    copies[0].wait()
    step = 64

    def widen(i, carry):
        rows = pl.ds(pl.multiple_of(i * step, step), step)
        g_ref[rows, :] = part_ref[rows, :].astype(F32)
        return carry

    lax.fori_loop(0, BLK * B // step, widen, 0, unroll=4)
    for c in copies[1:5]:
        c.wait()
    moment_ref[0:2, :] = rows_ref[...]
    moment_ref[2:4, :] = cols_ref[...]
    left_ref[0] = left_ref[0] * DECAY
    right_ref[0] = right_ref[0] * DECAY
    for c in copies[5:]:
        c.wait()


def in_hbm(*arrays):
    return [pltpu.with_memory_space_constraint(a, pltpu.HBM) for a in arrays]


def load(g, lroot, rroot, left, right, rows, cols):
    return pl.pallas_call(
        load_kernel,
        out_shape=(
            pltpu.VMEM((BLK * B, B), F32),
            pltpu.VMEM((CAP, B, B), BF16),
            pltpu.VMEM((CAP, B, B), BF16),
            pltpu.VMEM((CAP, B, B), F32),
            pltpu.VMEM((CAP, B, B), F32),
            pltpu.VMEM((4, B), F32),
        ),
        in_specs=[HB] * 7,
        out_specs=(VM,) * 6,
        scratch_shapes=[
            pltpu.VMEM((BLK * B, B), BF16),
            pltpu.VMEM((CAP, B), F32),
            pltpu.VMEM((CAP, B), F32),
            pltpu.SemaphoreType.DMA((9,)),
        ],
        compiler_params=pltpu.CompilerParams(vmem_limit_bytes=4 * MIB),
        cost_estimate=pl.CostEstimate(flops=0, bytes_accessed=8 * MIB, transcendentals=0),
        name="load",
    )(*in_hbm(g, lroot, rroot, left, right, rows, cols))


def slot_of_entry(owner_ref):
    o0, o1, o2 = owner_ref[0, 0], owner_ref[0, 1], owner_ref[0, 2]
    one = jnp.int32(1)
    zero = jnp.int32(0)
    s1 = jnp.where(o1 == o0, one, zero)
    s2 = jnp.where(o2 == o0, one, zero) + jnp.where(o2 == o1, one, zero)
    return (o0, o1, o2), (zero, s1, s2)


def rows_of_slots(owner_ref, row_ref, me):
    owners, slots = slot_of_entry(owner_ref)
    found = []
    for s in range(CAP):
        row, filled = jnp.int32(0), jnp.int32(0)
        for k in range(BLK):
            hit = (owners[k] == me) & (slots[k] == s)
            row = jnp.where(hit, row_ref[0, k], row)
            filled = jnp.where(hit, jnp.int32(1), filled)
        found.append((row, filled))
    return found


def entry_of_blocks(owner_ref, row_ref, me):
    owners, slots = slot_of_entry(owner_ref)
    found = []
    for b in range(BLK):
        mine, slot = jnp.int32(0), jnp.int32(0)
        for k in range(BLK):
            hit = row_ref[0, k] == b
            mine = jnp.where(hit & (owners[k] == me), jnp.int32(1), mine)
            slot = jnp.where(hit, slots[k], slot)
        found.append((mine, slot))
    return found


def thirds(x):
    parts = []
    for _ in range(3):
        part = x.astype(BF16).astype(F32)
        parts.append(part)
        x = x - part
    return parts


def product_kernel(
    owner_ref, row_ref, g_ref, o_ref, lroot_ref, rroot_ref, moment_ref, _,
    mine_ref, send_ref, psq_ref, hi_ref, lo_ref, sq_ref, rs_ref, colsum_ref, flag_ref, tick_ref, prod_ref,
):
    me = lax.axis_index("dp")
    tick_ref[...] = jnp.zeros((1, 128), F32)
    pieces = []
    for s, (row, filled) in enumerate(rows_of_slots(owner_ref, row_ref, me)):
        flag_ref[8 + s : 9 + s, :] = jnp.full((1, 128), filled, jnp.int32).astype(F32)
        rows = pl.ds(pl.multiple_of(row * B, B), B)
        block = scaled_sum(g_ref[rows, :], o_ref[rows, :])
        high = block.astype(BF16)
        hi_ref[s] = high
        lo_ref[s] = (block - high.astype(F32)).astype(BF16)
        half = jnp.dot(lroot_ref[s], high, preferred_element_type=F32).astype(BF16)
        prod = jnp.dot(half, rroot_ref[s], preferred_element_type=F32)
        prod_ref[s] = prod.astype(BF16)
        square = jnp.sum(lanes_sum(prod * prod), axis=0, keepdims=True)
        psq_ref[s : s + 1, :] = square
        pieces += thirds(jnp.concatenate([square] * 4, axis=1))
    own = entry_of_blocks(owner_ref, row_ref, me)
    at_one = me == 1
    for i in range(2):
        rows = pl.ds(pl.multiple_of((me + i) * B, B), B)
        s = scaled_sum(g_ref[rows, :], o_ref[rows, :])
        s = s * s
        sq_ref[i] = s
        rs_ref[i] = jnp.broadcast_to(jnp.sum(lanes_sum(s), axis=1, keepdims=True), (B, 128))
        colsum_ref[i : i + 1, :] = jnp.sum(s, axis=0, keepdims=True)
        for k in range(2):
            flag = jnp.where(at_one, own[i + 1][k], own[i][k])
            flag_ref[4 * k + i : 4 * k + i + 1, :] = jnp.full((1, 128), flag, jnp.int32).astype(F32)
    pieces += thirds(moment_ref[...]) + [jnp.zeros((TAIL - 18, B), F32)]
    send_ref[BLK * HALF :, :] = jnp.concatenate(pieces, axis=0).astype(BF16)
    for out, home in ((mine_ref, me), (send_ref, 1 - me)):
        for j in range(BLK):
            chunk = 3 * home + j
            block = lax.shift_right_logical(chunk, 1)
            slot = jnp.where(block == 0, own[0][1], jnp.where(block == 1, own[1][1], own[2][1]))
            rows = pl.ds(pl.multiple_of((chunk - 2 * block) * HALF, HALF), HALF)
            out[j * HALF : (j + 1) * HALF, :] = prod_ref[slot, rows, :]


def products(owner, row_block, g, o, lroot, rroot, moments, after):
    return pl.pallas_call(
        product_kernel,
        out_shape=(
            pltpu.VMEM((BLK * HALF, B), BF16),
            pltpu.VMEM((BLK * HALF + TAIL, B), BF16),
            pltpu.VMEM((CAP, 128), F32),
            pltpu.VMEM((CAP, B, B), BF16),
            pltpu.VMEM((CAP, B, B), BF16),
            pltpu.VMEM((2, B, B), F32),
            pltpu.VMEM((2, B, 128), F32),
            pltpu.VMEM((2, B), F32),
            pltpu.VMEM((16, 128), F32),
            pltpu.VMEM((1, 128), F32),
        ),
        in_specs=[SM, SM] + [VM] * 6,
        out_specs=(VM,) * 10,
        scratch_shapes=[pltpu.VMEM((CAP, B, B), BF16)],
        compiler_params=pltpu.CompilerParams(vmem_limit_bytes=12 * MIB),
        cost_estimate=pl.CostEstimate(
            flops=100 * B * B * B, bytes_accessed=8 * MIB, transcendentals=0
        ),
        name="products",
    )(owner, row_block, g, o, lroot, rroot, moments, after)


NT = (((1,), (1,)), ((), ()))
TN = (((0,), (0,)), ((), ()))


def gram(x, y, dims):
    return lax.dot_general(x, y, dims, preferred_element_type=F32)


def gram_kernel(
    hi_ref, lo_ref, left_ref, right_ref, flag_ref, _,
    gl_ref, gr_ref, vec_ref, left1_ref, right1_ref, tick_ref, cross_ref,
):
    tick_ref[...] = jnp.zeros((1, 128), F32)
    stats = ((gl_ref, NT), (gr_ref, TN))
    halves = (slice(0, HALF), slice(HALF, B))
    lower = ((0, 0), (1, 1), (1, 0))
    for s in range(CAP):
        hi, lo = hi_ref[s], lo_ref[s]
        for i, (out, dims) in enumerate(stats):
            cross_ref[2 * s + i] = gram(hi, lo, dims)
            parts = [hi[h, :] if dims is NT else hi[:, h] for h in halves]
            for p, q in lower:
                out[s, halves[p], halves[q]] = gram(parts[p], parts[q], dims)
    keep = 1.0 - (1.0 - DECAY) * flag_ref[9:10, 0:1]
    left1_ref[...] = keep * left_ref[1]
    right1_ref[...] = keep * right_ref[1]
    diagonal = lax.broadcasted_iota(jnp.int32, (128, 128), 0) == lax.broadcasted_iota(
        jnp.int32, (128, 128), 1
    )
    for s in range(CAP):
        for i, (out, _) in enumerate(stats):
            for p, q in lower:
                at = (halves[p], halves[q])
                flip = cross_ref[2 * s + i, halves[q], halves[p]].T
                out[s, *at] = out[s, *at] + cross_ref[2 * s + i, *at] + flip
            out[s, halves[0], halves[1]] = out[s, halves[1], halves[0]].T
            for p in range(4):
                at = slice(128 * p, 128 * (p + 1))
                line = jnp.where(diagonal, out[s, at, at], 0.0)
                vec_ref[2 * i + s : 2 * i + s + 1, at] = jnp.sum(line, axis=0, keepdims=True)


def grams(hi, lo, left, right, flag, after):
    return pl.pallas_call(
        gram_kernel,
        out_shape=(
            pltpu.VMEM((CAP, B, B), F32),
            pltpu.VMEM((CAP, B, B), F32),
            pltpu.VMEM((4, B), F32),
            pltpu.VMEM((B, B), F32),
            pltpu.VMEM((B, B), F32),
            pltpu.VMEM((1, 128), F32),
        ),
        in_specs=[VM] * 6,
        out_specs=(VM,) * 6,
        scratch_shapes=[pltpu.VMEM((2 * CAP, B, B), F32)],
        compiler_params=pltpu.CompilerParams(vmem_limit_bytes=12 * MIB),
        cost_estimate=pl.CostEstimate(
            flops=400 * B * B * B, bytes_accessed=12 * MIB, transcendentals=0
        ),
        name="grams",
    )(hi, lo, left, right, flag, after)


def finish_kernel(
    total_ref, gl_ref, gr_ref, sq_ref, rs_ref, colsum_ref, vec_ref, flag_ref,
    left_ref, right_ref, left1_ref, right1_ref, moment_ref, mine_ref, recv_ref, psq_ref,
    dir_hbm, nl_hbm, nr_hbm, nrows_hbm, ncols_hbm,
    nl_ref, nr_ref, dir_ref, nrows_ref, ncols_ref, sems, *, entries
):
    me = lax.axis_index("dp")
    total = jnp.sum(total_ref[...].reshape(-1, 128), axis=0, keepdims=True)
    total = jnp.sum(total, axis=1, keepdims=True)
    clip = lax.rsqrt(total * (1.0 / entries) + 1e-6) * (1.0 / SCALE)
    clip2 = clip * clip
    mix = (1.0 - DECAY) / B * clip2
    copies = []

    def send_out(src, dst, sem):
        copies.append(pltpu.make_async_copy(src, dst, sems.at[sem]))
        copies[-1].start()

    for s in range(CAP):
        filled = flag_ref[8 + s : 9 + s, 0:1]
        keep = 1.0 - (1.0 - DECAY) * filled
        add = mix * filled
        nrows_ref[s : s + 1, :] = keep * moment_ref[s : s + 1, :] + add * vec_ref[s : s + 1, :]
        ncols_ref[s : s + 1, :] = keep * moment_ref[2 + s : 3 + s, :] + add * vec_ref[2 + s : 3 + s, :]
        for i, (new, old, stat, hbm) in enumerate(
            (
                (nl_ref, (left_ref.at[0], left1_ref)[s], gl_ref, nl_hbm),
                (nr_ref, (right_ref.at[0], right1_ref)[s], gr_ref, nr_hbm),
            )
        ):
            for h in range(4):
                rows = slice(h * 128, (h + 1) * 128)
                new[s, rows, :] = old[rows, :] + add * stat[s, rows, :]
                send_out(new.at[s, rows, :], hbm.at[s, rows, :], 8 * s + 4 * i + h)
    send_out(nrows_ref, nrows_hbm, 16)
    send_out(ncols_ref, ncols_hbm, 17)
    factors, owns = [], []
    tail = recv_ref[BLK * HALF :, :].astype(F32)
    others = tail[6:10] + tail[10:14] + tail[14:18]
    for i in range(2):
        own = flag_ref[i : i + 1, 0:1] > 0.5
        first = flag_ref[4 + i : 5 + i, 0:1] < 0.5

        def pick(mine, theirs, k):
            return jnp.where(
                own,
                jnp.where(first, mine[k : k + 1, :], mine[k + 1 : k + 2, :]),
                jnp.where(first, theirs[k : k + 1, :], theirs[k + 1 : k + 2, :]),
            )

        old_rows = jnp.broadcast_to(pick(moment_ref, others, 0), (128, B)).T
        new_rows = DECAY * old_rows + mix * rs_ref[i]
        mean = jnp.sum(new_rows, axis=0, keepdims=True) * (1.0 / B)
        share = new_rows * (1.0 / mean)
        u = share * lax.rsqrt(share)
        v = jnp.sqrt(DECAY * pick(moment_ref, others, 2) + mix * colsum_ref[i : i + 1, :])
        acc = jnp.zeros((8, 128), F32)
        for j in range(4):
            cols = slice(128 * j, 128 * (j + 1))
            r = pl.reciprocal(u * v[:, cols] + 1e-8, approx=True)
            acc = acc + jnp.sum((sq_ref[i, :, cols] * r * r).reshape(B // 8, 8, 128), axis=0)
        adam = jnp.sum(jnp.sum(acc, axis=0, keepdims=True), axis=1, keepdims=True)
        adam = adam * clip2 * (1.0 / (B * B))
        theirs = jnp.concatenate(
            [tail[0:1] + tail[1:2] + tail[2:3], tail[3:4] + tail[4:5] + tail[5:6]], axis=0
        )
        psq = pick(psq_ref, theirs[:, 0:128], 0)
        psq = jnp.sum(psq, axis=1, keepdims=True) * clip2 * (1.0 / (B * B))
        factors.append(-clip * jnp.sqrt(adam) * lax.rsqrt(psq + 1e-6))
        owns.append(flag_ref[i : i + 1, 0:1])
    at_one = me == 1
    for j in range(BLK):
        rows = slice(j * HALF, (j + 1) * HALF)
        low, high = j // 2, (j + 1) // 2
        factor = jnp.where(at_one, factors[high], factors[low])
        own = jnp.where(at_one, owns[high], owns[low])
        piece = jnp.where(own > 0.5, mine_ref[rows, :].astype(F32), recv_ref[rows, :].astype(F32))
        dir_ref[rows, :] = (piece * factor).astype(BF16)
        send_out(dir_ref.at[rows, :], dir_hbm.at[rows, :], 18 + j)
    for c in copies:
        c.wait()


def finish(entries, *args):
    return pl.pallas_call(
        functools.partial(finish_kernel, entries=entries),
        out_shape=(
            jax.ShapeDtypeStruct((BLK * HALF, B), BF16),
            jax.ShapeDtypeStruct((CAP, B, B), F32),
            jax.ShapeDtypeStruct((CAP, B, B), F32),
            jax.ShapeDtypeStruct((CAP, B), F32),
            jax.ShapeDtypeStruct((CAP, B), F32),
        ),
        in_specs=[VM] * 16,
        out_specs=(HB,) * 5,
        scratch_shapes=[
            pltpu.VMEM((CAP, B, B), F32),
            pltpu.VMEM((CAP, B, B), F32),
            pltpu.VMEM((BLK * HALF, B), BF16),
            pltpu.VMEM((CAP, B), F32),
            pltpu.VMEM((CAP, B), F32),
            pltpu.SemaphoreType.DMA((21,)),
        ],
        compiler_params=pltpu.CompilerParams(vmem_limit_bytes=12 * MIB),
        cost_estimate=pl.CostEstimate(
            flops=16 * B * B, bytes_accessed=16 * MIB, transcendentals=0
        ),
        name="finish",
    )(*args)


def around(c, odd, size):
    return (((c + odd) ^ 1) - odd) % size


ROUNDS = (
    lambda z, y, x: (z, y, around(x, 0, 4)),
    lambda z, y, x: (z, y, around(x, 1, 4)),
)


def chip(z, y, x):
    return (z * 4 + y) * 4 + x


def mp_swap(v, peer):
    size = lax.axis_size("mp")
    pairs = [
        (chip(z, y, x), chip(*peer(z, y, x)))
        for z in range(8) for y in range(4) for x in range(4)
    ]
    return v + lax.ppermute(v, "mp", [p for p in pairs if max(p) < size])


def rest_chips(v):
    if lax.axis_size("mp") != 128:
        return v
    groups = [[chip(z, y, x) for z in range(8) for y in range(4)] for x in range(4)]
    many = jnp.broadcast_to(v, (len(groups[0]), 128))
    return lax.all_to_all(many, "mp", 0, 0, tiled=True, axis_index_groups=groups)


def on_device(
    grad_parts, owner, row_block, left_stats, right_stats, left_root, right_root, row_moment, col_moment
):
    entries = BLK * B * B * lax.axis_size("mp")
    o = lax.ppermute(grad_parts[0], "dp", SWAP)
    g, lroot, rroot, left, right, moments = load(
        grad_parts[0], left_root[0], right_root[0], left_stats[0], right_stats[0], row_moment[0], col_moment[0]
    )
    part = square_sum(g, o)
    mine, send, psq, hi, lo, sq, rs, colsum, flag, tick = products(owner, row_block, g, o, lroot, rroot, moments, part)
    recv = lax.ppermute(send, "dp", SWAP)
    part = mp_swap(part, ROUNDS[0]) + tick
    gl, gr, vec, left1, right1, tick = grams(hi, lo, left, right, flag, part)
    part = mp_swap(part, ROUNDS[1]) + tick
    total = rest_chips(part)
    direction, new_left, new_right, new_rows, new_cols = finish(
        entries, total, gl, gr, sq, rs, colsum, vec, flag, left, right, left1, right1, moments, mine, recv, psq
    )
    return (direction, new_left[None], new_right[None], new_rows[None], new_cols[None])


def solution(mesh):
    return jax.shard_map(
        on_device,
        mesh=mesh,
        in_specs=(
            P("dp", None, "mp"),
            P("mp", None),
            P("mp", None),
            P("mp", "dp", None, None),
            P("mp", "dp", None, None),
            P("mp", "dp", None, None),
            P("mp", "dp", None, None),
            P("mp", "dp", None),
            P("mp", "dp", None),
        ),
        out_specs=(
            P("dp", "mp"),
            P("mp", "dp", None, None),
            P("mp", "dp", None, None),
            P("mp", "dp", None),
            P("mp", "dp", None),
        ),
        check_vma=False,
    )
```
